32 devices in a mesh: sensor: 2 (over core), tm: 16 (over z, y, x).
Axes of the slice: x: 2, y: 2, z: 4, core: 2. Of those that a mesh axis runs over, the one named last changes fastest.
Arguments:
- readings: float32 [512, 128], P(('sensor', 'tm')), may hold values from -18 to 18
- noise_var: float32 [512, 128], P(('sensor', 'tm')), may hold values from 0.1 to 1
- sensor_weights: float32 [512, 64, 128], P(('sensor', 'tm')), may hold values from -0.1 to 1, as said below
- time_weights: float32 [512, 256, 128], P(('sensor', 'tm')), may hold values from -0.1 to 1, as said below
- window_index: int32 [512], P(('sensor', 'tm')), may hold values from 0 to 31
- sensor_kernel: float32 [4096, 4096], P('sensor'), may hold values from -1 to 1.5, as said below
- time_kernel: float32 [4096, 4096], P('tm'), may hold values from -1 to 1.5, as said below
Outputs:
- solution: float32 [512, 128], P(('sensor', 'tm'))
- residual: float32 [512, 128], P(('sensor', 'tm'))
The draws below stay inside these ranges and needn't reach their ends.
Inputs may be any that keep to these rules, and one draw needn't show every extreme that they name: Block b's readings interpolate from sensor rows 64 * window_index[b] to 64 * window_index[b] + 63 of the sensor rows that its device holds. `sensor_weights`: each reading's column holds the four cubic convolution weights of one position, in rows p - 1 to p + 2 for some p with 1 <= p <= 61; the other entries are zero. `time_weights`: each reading's column holds the four cubic convolution weights of one position, in rows p - 1 to p + 2 for some p with 1 <= p <= 253; the other entries are zero. `sensor_kernel`: symmetric and positive definite. `time_kernel`: symmetric and positive definite.
All inputs are finite; a program needn't handle non-finite values.
Results may differ from the reference program's by a relative error of at most 0.0003.
Values sent between devices are 32-bit elements; how exact they have to be, the bound alone decides.
A program may use at most 192 MiB of HBM per device.

```python
import math
import jax
import jax.numpy as jnp
from jax import lax

SENSORS = 4096
TIMES = 4096
SWIN = 64
RB = 128
BLK_DEV = 16
ITERS = 2
TIME_DEV = 256
WINS = 32
BLOCKS = 512
N_SENSOR = 2
N_TM = 16


def cubic_tile(key, window_len):
    key_anchor, key_fraction = jax.random.split(key)
    anchor = jax.random.randint(key_anchor, (BLOCKS, RB), 1, window_len - 2)
    fraction = jax.random.uniform(key_fraction, (BLOCKS, RB), jnp.float32)
    cube = fraction * fraction * fraction
    square = fraction * fraction
    stencil = (-0.5 * cube + square - 0.5 * fraction, 1.5 * cube - 2.5 * square + 1.0, -1.5 * cube + 2.0 * square + 0.5 * fraction, 0.5 * cube - 0.5 * square)
    positions = jnp.arange(window_len, dtype=jnp.int32)[None, :, None]
    first_row = (anchor - 1)[:, None, :]
    dense_tile = jnp.zeros((BLOCKS, window_len, RB), jnp.float32)
    for offset in range(4):
        dense_tile = dense_tile + jnp.where(positions == first_row + offset, stencil[offset][:, None, :], 0.0)
    return dense_tile


def symmetric_kernel(key, matrix_order):
    key_entries, key_diagonal = jax.random.split(key)
    spread = 0.735
    matrix = jax.random.uniform(key_entries, (matrix_order, matrix_order), jnp.float32, -1.0, 1.0)
    symmetric = (matrix + matrix.T) * (0.5 * spread / math.sqrt(matrix_order))
    diagonal = 1.0 + 0.5 * jax.random.uniform(key_diagonal, (matrix_order,), jnp.float32)
    identity = jnp.eye(matrix_order, dtype=jnp.float32)
    return symmetric * (1.0 - identity) + identity * diagonal[None, :]


def draw_readings(key, part):
    position = jnp.arange(BLOCKS, dtype=jnp.float32)[:, None] / max(BLOCKS - 1, 1)
    raw_values = jnp.clip(jax.random.normal(key, (BLOCKS, RB), jnp.float32), -6.0, 6.0)
    return raw_values * (1.0 + 2.0 * position)


def draw_sensor_weights(key, part):
    return cubic_tile(jax.random.fold_in(key, 11), SWIN)


def draw_time_weights(key, part):
    return cubic_tile(jax.random.fold_in(key, 23), TIME_DEV)


def draw_sensor_kernel(key, part):
    return symmetric_kernel(jax.random.fold_in(key, 31), SENSORS)


def draw_time_kernel(key, part):
    return symmetric_kernel(jax.random.fold_in(key, 47), TIMES)


def plant(array, own_key, least, largest):
    longest = array.shape.index(max(array.shape))
    spots = []
    for shift in (0, 1):
        where = [jax.random.randint(jax.random.fold_in(own_key, axis), (), 0, length) for axis, length in enumerate(array.shape)]
        where[longest] = (where[longest] + shift) % array.shape[longest]
        spots.append(tuple(where))
    return array.at[spots[0]].set(least).at[spots[1]].set(largest)


def levels(stream_key, extent, pieces, low, top_value):
    def one(dim, shards_of):
        heights = jax.random.uniform(jax.random.fold_in(jax.random.fold_in(stream_key, 6), dim), (shards_of,), jnp.float32, low / len(pieces), top_value / len(pieces))
        return jnp.repeat(jnp.exp(heights), extent[dim] // shards_of).reshape((-1,) + (1,) * (len(extent) - dim - 1))

    factor_of = one(*pieces[0])
    for cut in pieces[1:]:
        factor_of = factor_of * one(*cut)
    return factor_of


def setup_inputs(seed: int = 0) -> dict:
    splits = jax.random.split(jax.random.key(seed), 8)
    return {
        "readings": draw_readings(jax.random.fold_in(splits[7], 71), 0),
        "noise_var": jnp.clip(jnp.exp(math.log(1.0) - 2.3025851 * jax.random.uniform(splits[1], (BLOCKS, RB), jnp.float32) ** levels(splits[1], (BLOCKS, RB), ((0, 32),), -0.2, 0.2)), 0.1, 1.0),
        "sensor_weights": draw_sensor_weights(jax.random.fold_in(splits[7], 71), 0),
        "time_weights": draw_time_weights(jax.random.fold_in(splits[7], 71), 0),
        "window_index": plant(jax.random.randint(splits[4], (BLOCKS,), 0, WINS), jax.random.fold_in(splits[4], 1), 0, WINS - 1).astype(jnp.int32),
        "sensor_kernel": draw_sensor_kernel(jax.random.fold_in(splits[7], 71), 0),
        "time_kernel": draw_time_kernel(jax.random.fold_in(splits[7], 71), 0),
    }


PRECISE = lax.Precision.HIGHEST


def reference(readings, noise_var, sensor_weights, time_weights, window_index, sensor_kernel, time_kernel):
    lead = (N_SENSOR, N_TM, BLK_DEV)
    onehot = (window_index.reshape(lead)[..., None] == jnp.arange(WINS, dtype=jnp.int32)).astype(jnp.float32)
    sensor_tile = sensor_weights.reshape(lead + (SWIN, RB))
    time_tile = time_weights.reshape(lead + (TIME_DEV, RB))
    noise_blocks = noise_var.reshape(lead + (RB,))

    kernel_grid = sensor_kernel.reshape(N_SENSOR, WINS, SWIN, N_SENSOR, WINS, SWIN)
    sensor_ids = jnp.arange(N_SENSOR, dtype=jnp.int32)[:, None]
    window_ids = jnp.arange(WINS, dtype=jnp.int32)[None, :]
    window_kernel = kernel_grid[sensor_ids, window_ids, :, sensor_ids, window_ids, :]
    block_kernel = jnp.einsum('stbw,swik->stbik', onehot, window_kernel, precision=PRECISE)
    sensor_quad = jnp.sum(sensor_tile * jnp.einsum('stbik,stbkr->stbir', block_kernel, sensor_tile, precision=PRECISE), axis=3)
    time_grid = time_kernel.reshape(N_TM, TIME_DEV, N_TM, TIME_DEV)
    time_ids = jnp.arange(N_TM, dtype=jnp.int32)
    time_square = time_grid[time_ids, :, time_ids, :]
    time_quad = jnp.sum(time_tile * jnp.einsum('tjl,stblr->stbjr', time_square, time_tile, precision=PRECISE), axis=3)
    inverse = 1.0 / (sensor_quad * time_quad + noise_blocks)

    def operator_apply(vector):
        scaled = vector[:, :, :, None, :] * time_tile
        contrib = jnp.einsum('stbir,stbjr->stbij', sensor_tile, scaled, precision=PRECISE)
        grid_field = jnp.einsum('stbw,stbij->switj', onehot, contrib, precision=PRECISE).reshape(SENSORS, TIMES)
        left_product = jnp.dot(sensor_kernel, grid_field, precision=PRECISE, preferred_element_type=jnp.float32)
        smooth = jnp.dot(left_product, time_kernel.T, precision=PRECISE, preferred_element_type=jnp.float32)
        smooth = smooth.reshape(N_SENSOR, WINS, SWIN, N_TM, TIME_DEV)
        gathered = jnp.einsum('stbw,switj->stbij', onehot, smooth, precision=PRECISE)
        interp_cols = jnp.einsum('stbij,stbjr->stbir', gathered, time_tile, precision=PRECISE)
        return jnp.sum(sensor_tile * interp_cols, axis=3) + noise_blocks * vector

    residual = readings.reshape(lead + (RB,))
    solution = jnp.zeros_like(residual)
    precond = inverse * residual
    direction = precond
    inner_now = jnp.sum(residual * precond)
    for iteration in range(ITERS):
        image_vec = operator_apply(direction)
        step_size = inner_now / jnp.sum(direction * image_vec)
        solution = solution + step_size * direction
        residual = residual - step_size * image_vec
        if iteration + 1 < ITERS:
            precond = inverse * residual
            inner_next = jnp.sum(residual * precond)
            direction = precond + (inner_next / inner_now) * direction
            inner_now = inner_next
    return solution.reshape(BLOCKS, RB), residual.reshape(BLOCKS, RB)
```

```python
import functools

import jax
import jax.numpy as jnp
from jax import lax
from jax.experimental import pallas as pl
from jax.experimental.pallas import tpu as pltpu
from jax.sharding import PartitionSpec as P

PRECISE = lax.Precision.HIGHEST
F32 = jnp.float32
BF16 = jnp.bfloat16
TAPS = 4
FIELDS = 11
AXES = ("sensor", "tm")


def split(x):
    hi = x.astype(BF16)
    return hi, (x - hi.astype(F32)).astype(BF16)


def dense(taps, first, rows):
    place = lax.broadcasted_iota(jnp.int32, (rows, first.shape[-1]), 0) - first
    out = jnp.where(place == TAPS - 1, taps[TAPS - 1], 0.0)
    for k in range(TAPS - 2, -1, -1):
        out = jnp.where(place == k, taps[k], out)
    return out


def compact_body(group, win_ref, sensor_ref, time_ref, pack_ref):
    step = pl.program_id(0)
    for g in range(group):
        row = pl.ds(step * group + g, 1)
        for ref, taps_at, first_at in ((time_ref, 0, 8), (sensor_ref, TAPS, 9)):
            tile = ref[g]
            ids = lax.broadcasted_iota(jnp.int32, tile.shape, 0)
            first = jnp.min(
                jnp.where(tile != 0.0, ids, tile.shape[0]), axis=0, keepdims=True
            )
            place = ids - first
            for k in range(TAPS):
                pack_ref[taps_at + k, row, :] = jnp.sum(
                    jnp.where(place == k, tile, 0.0), axis=0, keepdims=True
                )
            pack_ref[first_at, row, :] = first.astype(F32)
        window = win_ref[step * group + g]
        pack_ref[10, row, :] = jnp.full((1, tile.shape[1]), window, jnp.int32).astype(F32)


def compact(window_index, sensor_weights, time_weights):
    blocks, win_rows, readings = sensor_weights.shape
    time_dev = time_weights.shape[1]
    group = 4
    return pl.pallas_call(
        functools.partial(compact_body, group),
        grid_spec=pltpu.PrefetchScalarGridSpec(
            num_scalar_prefetch=1,
            grid=(blocks // group,),
            in_specs=[
                pl.BlockSpec((group, win_rows, readings), lambda i, w: (i, 0, 0)),
                pl.BlockSpec((group, time_dev, readings), lambda i, w: (i, 0, 0)),
            ],
            out_specs=pl.BlockSpec((FIELDS, blocks, readings), lambda i, w: (0, 0, 0)),
        ),
        out_shape=jax.ShapeDtypeStruct((FIELDS, blocks, readings), F32),
        name="compact",
    )(window_index, sensor_weights, time_weights)


def inverse_body(group, place_ref, *refs):
    squares = refs[:group]
    time_square, sensor_ref, time_ref, noise_ref, inverse_ref = refs[group:]
    step = pl.program_id(0)
    for g in range(group):
        block = step * group + g
        row = pl.ds(block, 1)
        weights = sensor_ref[g]
        odd = (place_ref[block] % 2).astype(F32)
        both = jnp.concatenate([weights * (1.0 - odd), weights * odd], axis=0)
        mixed = jnp.dot(squares[g][...], both, precision=PRECISE, preferred_element_type=F32)
        sensor_quad = jnp.sum(weights * mixed, axis=0, keepdims=True)
        taps = time_ref[g]
        mixed = jnp.dot(time_square[...], taps, precision=PRECISE, preferred_element_type=F32)
        time_quad = jnp.sum(taps * mixed, axis=0, keepdims=True)
        inverse_ref[row, :] = 1.0 / (sensor_quad * time_quad + noise_ref[row, :])


def inverse_of(noise_var, sensor_weights, time_weights, window_index, sensor_kernel, time_kernel):
    blocks, win_rows, readings = sensor_weights.shape
    time_dev = time_weights.shape[1]
    sensor_dev = sensor_kernel.shape[0]
    group = 4
    place = jnp.concatenate(
        [
            window_index,
            lax.axis_index("sensor")[None].astype(jnp.int32),
            lax.axis_index("tm")[None].astype(jnp.int32),
        ]
    )

    def square(g):
        def where(i, p):
            window = p[i * group + g]
            return window, (p[blocks] * sensor_dev + window * win_rows) // (2 * win_rows)

        return pl.BlockSpec((win_rows, 2 * win_rows), where)

    return pl.pallas_call(
        functools.partial(inverse_body, group),
        grid_spec=pltpu.PrefetchScalarGridSpec(
            num_scalar_prefetch=1,
            grid=(blocks // group,),
            in_specs=[square(g) for g in range(group)]
            + [
                pl.BlockSpec((time_dev, time_dev), lambda i, p: (0, p[blocks + 1])),
                pl.BlockSpec((group, win_rows, readings), lambda i, p: (i, 0, 0)),
                pl.BlockSpec((group, time_dev, readings), lambda i, p: (i, 0, 0)),
                pl.BlockSpec((blocks, readings), lambda i, p: (0, 0)),
            ],
            out_specs=pl.BlockSpec((blocks, readings), lambda i, p: (0, 0)),
        ),
        out_shape=jax.ShapeDtypeStruct((blocks, readings), F32),
        cost_estimate=pl.CostEstimate(
            flops=12 * blocks * time_dev * time_dev * readings,
            bytes_accessed=4 * blocks * time_dev * readings * 4,
            transcendentals=0,
        ),
        name="inverse",
    )(place, *([sensor_kernel] * group), time_kernel, sensor_weights, time_weights, noise_var)


def times_body(pack_ref, kernel_ref, mixed_ref):
    time_dev = kernel_ref.shape[0]
    blocks, readings = pack_ref.shape[2:]
    k_hi, k_lo = split(kernel_ref[...])
    for b in range(0, blocks, 2):
        tiles = []
        for c in (b, b + 1):
            row = slice(c, c + 1)
            taps = [pack_ref[0, k, row, :] for k in range(TAPS)]
            tiles.append(dense(taps, pack_ref[0, 8, row, :].astype(jnp.int32), time_dev))
        w_hi, w_lo = split(jnp.concatenate(tiles, axis=1))
        dot = functools.partial(jnp.dot, preferred_element_type=F32)
        hi, lo = split(dot(k_hi, w_hi) + (dot(k_hi, w_lo) + dot(k_lo, w_hi)))
        for n in range(2):
            part = slice(n * readings, (n + 1) * readings)
            mixed_ref[b + n, :, :readings] = hi[:, part]
            mixed_ref[b + n, :, readings:] = lo[:, part]


def mix_times(pack, time_kernel):
    n_tm, _, blocks, readings = pack.shape
    time_dev = time_kernel.shape[0]
    return pl.pallas_call(
        times_body,
        grid=(n_tm,),
        in_specs=[
            pl.BlockSpec((1, FIELDS, blocks, readings), lambda i: (i, 0, 0, 0)),
            pl.BlockSpec((time_dev, time_dev), lambda i: (0, i)),
        ],
        out_specs=pl.BlockSpec((blocks, time_dev, 2 * readings), lambda i: (i, 0, 0)),
        out_shape=jax.ShapeDtypeStruct((n_tm * blocks, time_dev, 2 * readings), BF16),
        compiler_params=pltpu.CompilerParams(vmem_limit_bytes=40 << 20),
        cost_estimate=pl.CostEstimate(
            flops=6 * n_tm * blocks * time_dev * time_dev * readings,
            bytes_accessed=4 * n_tm * blocks * time_dev * readings,
            transcendentals=0,
        ),
        name="mix_times",
    )(pack, time_kernel)


def field_body(win_rows, win_ref, pack_ref, value_ref, mixed_ref, field_ref):
    step = pl.program_id(0)
    blocks, readings = pack_ref.shape[2:]

    @pl.when(step == 0)
    def _():
        field_ref[...] = jnp.zeros_like(field_ref)

    for b in range(blocks):
        row = slice(b, b + 1)
        value = value_ref[0, row, :]
        taps = [pack_ref[0, TAPS + k, row, :] * value for k in range(TAPS)]
        hi, lo = split(dense(taps, pack_ref[0, 9, row, :].astype(jnp.int32), win_rows))
        left = jnp.concatenate(
            [
                jnp.concatenate([hi, hi], axis=1),
                jnp.concatenate([lo, jnp.zeros_like(lo)], axis=1),
            ],
            axis=0,
        )
        out = lax.dot_general(
            left, mixed_ref[b], (((1,), (1,)), ((), ())), preferred_element_type=F32
        )
        start = pl.multiple_of(win_ref[step * blocks + b] * win_rows, win_rows)
        field_ref[pl.ds(start, win_rows), :] += out[:win_rows] + out[win_rows:]


def field_of(windows, pack, values, mixed, sensor_dev, win_rows):
    n_tm, _, blocks, readings = pack.shape
    time_dev = mixed.shape[1]
    return pl.pallas_call(
        functools.partial(field_body, win_rows),
        grid_spec=pltpu.PrefetchScalarGridSpec(
            num_scalar_prefetch=1,
            grid=(n_tm,),
            in_specs=[
                pl.BlockSpec((1, FIELDS, blocks, readings), lambda i, w: (i, 0, 0, 0)),
                pl.BlockSpec((1, blocks, readings), lambda i, w: (i, 0, 0)),
                pl.BlockSpec((blocks, time_dev, 2 * readings), lambda i, w: (i, 0, 0)),
            ],
            out_specs=pl.BlockSpec((sensor_dev, time_dev), lambda i, w: (0, 0)),
        ),
        out_shape=jax.ShapeDtypeStruct((sensor_dev, time_dev), F32),
        compiler_params=pltpu.CompilerParams(vmem_limit_bytes=40 << 20),
        name="field",
    )(windows, pack, values, mixed)


def image_body(group, chunk, win_ref, *refs):
    kernels = refs[:group]
    field_ref, sensor_ref, time_ref, noise_ref, value_ref, image_ref, halves = refs[group:]
    step = pl.program_id(0)
    time_dev = field_ref.shape[1]
    win_rows = sensor_ref.shape[1]
    sensors = field_ref.shape[0]
    dot = functools.partial(jnp.dot, preferred_element_type=F32)

    @pl.when(step == 0)
    def _():
        for k in range(0, sensors, chunk):
            hi, lo = split(field_ref[k : k + chunk, :])
            halves[k : k + chunk, :time_dev] = hi
            halves[k : k + chunk, time_dev:] = lo

    total = jnp.zeros((group * win_rows, 2 * time_dev), F32)
    extra = jnp.zeros((group * win_rows, time_dev), F32)
    for k in range(0, sensors, chunk):
        left = jnp.concatenate([ref[:, k : k + chunk] for ref in kernels], axis=0)
        hi, lo = split(left)
        total = total + dot(hi, halves[k : k + chunk, :])
        extra = extra + dot(lo, halves[k : k + chunk, :time_dev])
    smooth = total[:, :time_dev] + (total[:, time_dev:] + extra)
    for g in range(group):
        row = pl.ds(step * group + g, 1)
        interp = jnp.dot(
            smooth[g * win_rows : (g + 1) * win_rows],
            time_ref[g],
            precision=PRECISE,
            preferred_element_type=F32,
        )
        image_ref[row, :] = (
            jnp.sum(sensor_ref[g] * interp, axis=0, keepdims=True)
            + noise_ref[row, :] * value_ref[row, :]
        )


def image_of(window_index, sensor_kernel, field, sensor_weights, time_weights, noise_var, value):
    blocks, win_rows, readings = sensor_weights.shape
    sensors, time_dev = field.shape
    group = 4
    chunk = 512

    def rows(g):
        return pl.BlockSpec((win_rows, sensors), lambda i, w: (w[i * group + g], 0))

    return pl.pallas_call(
        functools.partial(image_body, group, chunk),
        grid_spec=pltpu.PrefetchScalarGridSpec(
            num_scalar_prefetch=1,
            grid=(blocks // group,),
            in_specs=[rows(g) for g in range(group)]
            + [
                pl.BlockSpec((sensors, time_dev), lambda i, w: (0, 0)),
                pl.BlockSpec((group, win_rows, readings), lambda i, w: (i, 0, 0)),
                pl.BlockSpec((group, time_dev, readings), lambda i, w: (i, 0, 0)),
                pl.BlockSpec((blocks, readings), lambda i, w: (0, 0)),
                pl.BlockSpec((blocks, readings), lambda i, w: (0, 0)),
            ],
            out_specs=pl.BlockSpec((blocks, readings), lambda i, w: (0, 0)),
            scratch_shapes=[pltpu.VMEM((sensors, 2 * time_dev), BF16)],
        ),
        out_shape=jax.ShapeDtypeStruct((blocks, readings), F32),
        compiler_params=pltpu.CompilerParams(vmem_limit_bytes=48 << 20),
        name="image",
    )(
        window_index,
        *([sensor_kernel] * group),
        field,
        sensor_weights,
        time_weights,
        noise_var,
        value,
    )


def on_device(
    n_sensor,
    n_tm,
    readings,
    noise_var,
    sensor_weights,
    time_weights,
    window_index,
    sensor_kernel,
    time_kernel,
):
    sensor_dev = sensor_kernel.shape[0]
    win_rows = sensor_weights.shape[1]
    blocks = readings.shape[0]
    mine = lax.axis_index("sensor")

    def everywhere(x):
        return lax.all_gather(x, AXES, axis=0, tiled=False)

    pack = lax.all_gather(
        compact(window_index, sensor_weights, time_weights), "tm", axis=0, tiled=False
    )
    inverse = inverse_of(
        noise_var, sensor_weights, time_weights, window_index, sensor_kernel, time_kernel
    )
    start = everywhere(jnp.stack([readings, inverse]))
    windows = pack[:, 10, :, 0].astype(jnp.int32).reshape(-1)
    mixed = mix_times(pack, time_kernel)
    residual_all, inverse_all = start[:, 0], start[:, 1]
    direction_all = inverse_all * residual_all
    direction = inverse * readings
    inner = jnp.sum(residual_all * direction_all)

    def operator_apply(values_all, values):
        own = lax.dynamic_slice_in_dim(values_all, mine * n_tm, n_tm, 0)
        field = field_of(windows, pack, own, mixed, sensor_dev, win_rows)
        field = lax.all_gather(field, "sensor", axis=0, tiled=True)
        return image_of(
            window_index, sensor_kernel, field, sensor_weights, time_weights, noise_var, values
        )

    image = operator_apply(direction_all, direction)
    image_all = everywhere(image)
    step_size = inner / jnp.sum(direction_all * image_all)
    solution = step_size * direction
    residual = readings - step_size * image
    residual_all = residual_all - step_size * image_all
    precond_all = inverse_all * residual_all
    inner_next = jnp.sum(residual_all * precond_all)
    ratio = inner_next / inner
    direction = inverse * residual + ratio * direction
    direction_all = precond_all + ratio * direction_all
    inner = inner_next

    image = operator_apply(direction_all, direction)
    curve = jnp.sum(everywhere(jnp.sum(direction * image, axis=0, keepdims=True)))
    step_size = inner / curve
    return solution + step_size * direction, residual - step_size * image


def solution(mesh):
    in_specs = (
        P(("sensor", "tm"), None),
        P(("sensor", "tm"), None),
        P(("sensor", "tm"), None, None),
        P(("sensor", "tm"), None, None),
        P(("sensor", "tm")),
        P("sensor", None),
        P("tm", None),
    )
    out_specs = (P(("sensor", "tm"), None), P(("sensor", "tm"), None))
    return jax.shard_map(
        functools.partial(on_device, mesh.shape["sensor"], mesh.shape["tm"]),
        mesh=mesh,
        in_specs=in_specs,
        out_specs=out_specs,
        check_vma=False,
    )
```

```python
import functools

import jax
import jax.numpy as jnp
from jax import lax
from jax.experimental import pallas as pl
from jax.experimental.pallas import tpu as pltpu
from jax.sharding import PartitionSpec as P

PRECISE = lax.Precision.HIGHEST
F32 = jnp.float32
BF16 = jnp.bfloat16
TAPS = 4
FIELDS = 11


def split(x):
    hi = x.astype(BF16)
    return hi, (x - hi.astype(F32)).astype(BF16)


def dense(taps, first, rows):
    place = lax.broadcasted_iota(jnp.int32, (rows, first.shape[-1]), 0) - first
    out = jnp.where(place == TAPS - 1, taps[TAPS - 1], 0.0)
    for k in range(TAPS - 2, -1, -1):
        out = jnp.where(place == k, taps[k], out)
    return out


def compact_body(group, win_ref, sensor_ref, time_ref, pack_ref):
    step = pl.program_id(0)
    for g in range(group):
        row = pl.ds(step * group + g, 1)
        for ref, taps_at, first_at in ((time_ref, 0, 8), (sensor_ref, TAPS, 9)):
            tile = ref[g]
            ids = lax.broadcasted_iota(jnp.int32, tile.shape, 0)
            first = jnp.min(
                jnp.where(tile != 0.0, ids, tile.shape[0]), axis=0, keepdims=True
            )
            place = ids - first
            for k in range(TAPS):
                pack_ref[taps_at + k, row, :] = jnp.sum(
                    jnp.where(place == k, tile, 0.0), axis=0, keepdims=True
                )
            pack_ref[first_at, row, :] = first.astype(F32)
        window = win_ref[step * group + g]
        pack_ref[10, row, :] = jnp.full((1, tile.shape[1]), window, jnp.int32).astype(F32)


def compact(window_index, sensor_weights, time_weights):
    blocks, win_rows, readings = sensor_weights.shape
    time_dev = time_weights.shape[1]
    group = 4
    return pl.pallas_call(
        functools.partial(compact_body, group),
        grid_spec=pltpu.PrefetchScalarGridSpec(
            num_scalar_prefetch=1,
            grid=(blocks // group,),
            in_specs=[
                pl.BlockSpec((group, win_rows, readings), lambda i, w: (i, 0, 0)),
                pl.BlockSpec((group, time_dev, readings), lambda i, w: (i, 0, 0)),
            ],
            out_specs=pl.BlockSpec((FIELDS, blocks, readings), lambda i, w: (0, 0, 0)),
        ),
        out_shape=jax.ShapeDtypeStruct((FIELDS, blocks, readings), F32),
        name="compact",
    )(window_index, sensor_weights, time_weights)


def inverse_body(group, place_ref, *refs):
    squares = refs[:group]
    time_square, sensor_ref, time_ref, noise_ref, inverse_ref = refs[group:]
    step = pl.program_id(0)
    for g in range(group):
        block = step * group + g
        row = pl.ds(block, 1)
        weights = sensor_ref[g]
        odd = (place_ref[block] % 2).astype(F32)
        both = jnp.concatenate([weights * (1.0 - odd), weights * odd], axis=0)
        mixed = jnp.dot(squares[g][...], both, precision=PRECISE, preferred_element_type=F32)
        sensor_quad = jnp.sum(weights * mixed, axis=0, keepdims=True)
        taps = time_ref[g]
        mixed = jnp.dot(time_square[...], taps, precision=PRECISE, preferred_element_type=F32)
        time_quad = jnp.sum(taps * mixed, axis=0, keepdims=True)
        inverse_ref[row, :] = 1.0 / (sensor_quad * time_quad + noise_ref[row, :])


def inverse_of(noise_var, sensor_weights, time_weights, window_index, sensor_kernel, time_kernel):
    blocks, win_rows, readings = sensor_weights.shape
    time_dev = time_weights.shape[1]
    sensor_dev = sensor_kernel.shape[0]
    group = 4
    place = jnp.concatenate(
        [
            window_index,
            lax.axis_index("sensor")[None].astype(jnp.int32),
            lax.axis_index("tm")[None].astype(jnp.int32),
        ]
    )

    def square(g):
        def where(i, p):
            window = p[i * group + g]
            return window, (p[blocks] * sensor_dev + window * win_rows) // (2 * win_rows)

        return pl.BlockSpec((win_rows, 2 * win_rows), where)

    return pl.pallas_call(
        functools.partial(inverse_body, group),
        grid_spec=pltpu.PrefetchScalarGridSpec(
            num_scalar_prefetch=1,
            grid=(blocks // group,),
            in_specs=[square(g) for g in range(group)]
            + [
                pl.BlockSpec((time_dev, time_dev), lambda i, p: (0, p[blocks + 1])),
                pl.BlockSpec((group, win_rows, readings), lambda i, p: (i, 0, 0)),
                pl.BlockSpec((group, time_dev, readings), lambda i, p: (i, 0, 0)),
                pl.BlockSpec((blocks, readings), lambda i, p: (0, 0)),
            ],
            out_specs=pl.BlockSpec((blocks, readings), lambda i, p: (0, 0)),
        ),
        out_shape=jax.ShapeDtypeStruct((blocks, readings), F32),
        cost_estimate=pl.CostEstimate(
            flops=12 * blocks * time_dev * time_dev * readings,
            bytes_accessed=4 * blocks * time_dev * readings * 4,
            transcendentals=0,
        ),
        name="inverse",
    )(place, *([sensor_kernel] * group), time_kernel, sensor_weights, time_weights, noise_var)


def times_body(pack_ref, kernel_ref, mixed_ref):
    time_dev = kernel_ref.shape[0]
    blocks, readings = pack_ref.shape[2:]
    k_hi, k_lo = split(kernel_ref[...])
    for b in range(0, blocks, 2):
        tiles = []
        for c in (b, b + 1):
            row = slice(c, c + 1)
            taps = [pack_ref[0, k, row, :] for k in range(TAPS)]
            tiles.append(dense(taps, pack_ref[0, 8, row, :].astype(jnp.int32), time_dev))
        w_hi, w_lo = split(jnp.concatenate(tiles, axis=1))
        dot = functools.partial(jnp.dot, preferred_element_type=F32)
        hi, lo = split(dot(k_hi, w_hi) + (dot(k_hi, w_lo) + dot(k_lo, w_hi)))
        for n in range(2):
            part = slice(n * readings, (n + 1) * readings)
            mixed_ref[b + n, :, :readings] = hi[:, part]
            mixed_ref[b + n, :, readings:] = lo[:, part]


def mix_times(pack, time_kernel):
    n_tm, _, blocks, readings = pack.shape
    time_dev = time_kernel.shape[0]
    return pl.pallas_call(
        times_body,
        grid=(n_tm,),
        in_specs=[
            pl.BlockSpec((1, FIELDS, blocks, readings), lambda i: (i, 0, 0, 0)),
            pl.BlockSpec((time_dev, time_dev), lambda i: (0, i)),
        ],
        out_specs=pl.BlockSpec((blocks, time_dev, 2 * readings), lambda i: (i, 0, 0)),
        out_shape=jax.ShapeDtypeStruct((n_tm * blocks, time_dev, 2 * readings), BF16),
        compiler_params=pltpu.CompilerParams(vmem_limit_bytes=40 << 20),
        cost_estimate=pl.CostEstimate(
            flops=6 * n_tm * blocks * time_dev * time_dev * readings,
            bytes_accessed=4 * n_tm * blocks * time_dev * readings,
            transcendentals=0,
        ),
        name="mix_times",
    )(pack, time_kernel)


def field_body(win_rows, win_ref, pack_ref, value_ref, mixed_ref, field_ref):
    step = pl.program_id(0)
    blocks, readings = pack_ref.shape[2:]

    @pl.when(step == 0)
    def _():
        field_ref[...] = jnp.zeros_like(field_ref)

    for b in range(blocks):
        row = slice(b, b + 1)
        value = value_ref[0, row, :]
        taps = [pack_ref[0, TAPS + k, row, :] * value for k in range(TAPS)]
        hi, lo = split(dense(taps, pack_ref[0, 9, row, :].astype(jnp.int32), win_rows))
        left = jnp.concatenate(
            [
                jnp.concatenate([hi, hi], axis=1),
                jnp.concatenate([lo, jnp.zeros_like(lo)], axis=1),
            ],
            axis=0,
        )
        out = lax.dot_general(
            left, mixed_ref[b], (((1,), (1,)), ((), ())), preferred_element_type=F32
        )
        start = pl.multiple_of(win_ref[step * blocks + b] * win_rows, win_rows)
        field_ref[pl.ds(start, win_rows), :] += out[:win_rows] + out[win_rows:]


def field_of(windows, pack, values, mixed, sensor_dev, win_rows):
    n_tm, _, blocks, readings = pack.shape
    time_dev = mixed.shape[1]
    return pl.pallas_call(
        functools.partial(field_body, win_rows),
        grid_spec=pltpu.PrefetchScalarGridSpec(
            num_scalar_prefetch=1,
            grid=(n_tm,),
            in_specs=[
                pl.BlockSpec((1, FIELDS, blocks, readings), lambda i, w: (i, 0, 0, 0)),
                pl.BlockSpec((1, blocks, readings), lambda i, w: (i, 0, 0)),
                pl.BlockSpec((blocks, time_dev, 2 * readings), lambda i, w: (i, 0, 0)),
            ],
            out_specs=pl.BlockSpec((sensor_dev, time_dev), lambda i, w: (0, 0)),
        ),
        out_shape=jax.ShapeDtypeStruct((sensor_dev, time_dev), F32),
        compiler_params=pltpu.CompilerParams(vmem_limit_bytes=40 << 20),
        name="field",
    )(windows, pack, values, mixed)


def image_body(group, chunk, win_ref, *refs):
    kernels = refs[:group]
    field_ref, sensor_ref, time_ref, noise_ref, value_ref, image_ref, halves = refs[group:]
    step = pl.program_id(0)
    time_dev = field_ref.shape[1]
    win_rows = sensor_ref.shape[1]
    sensors = field_ref.shape[0]
    dot = functools.partial(jnp.dot, preferred_element_type=F32)

    @pl.when(step == 0)
    def _():
        for k in range(0, sensors, chunk):
            hi, lo = split(field_ref[k : k + chunk, :])
            halves[k : k + chunk, :time_dev] = hi
            halves[k : k + chunk, time_dev:] = lo

    total = jnp.zeros((group * win_rows, 2 * time_dev), F32)
    extra = jnp.zeros((group * win_rows, time_dev), F32)
    for k in range(0, sensors, chunk):
        left = jnp.concatenate([ref[:, k : k + chunk] for ref in kernels], axis=0)
        hi, lo = split(left)
        total = total + dot(hi, halves[k : k + chunk, :])
        extra = extra + dot(lo, halves[k : k + chunk, :time_dev])
    smooth = total[:, :time_dev] + (total[:, time_dev:] + extra)
    for g in range(group):
        row = pl.ds(step * group + g, 1)
        interp = jnp.dot(
            smooth[g * win_rows : (g + 1) * win_rows],
            time_ref[g],
            precision=PRECISE,
            preferred_element_type=F32,
        )
        image_ref[row, :] = (
            jnp.sum(sensor_ref[g] * interp, axis=0, keepdims=True)
            + noise_ref[row, :] * value_ref[row, :]
        )


def image_of(window_index, sensor_kernel, field, sensor_weights, time_weights, noise_var, value):
    blocks, win_rows, readings = sensor_weights.shape
    sensors, time_dev = field.shape
    group = 4
    chunk = 512

    def rows(g):
        return pl.BlockSpec((win_rows, sensors), lambda i, w: (w[i * group + g], 0))

    return pl.pallas_call(
        functools.partial(image_body, group, chunk),
        grid_spec=pltpu.PrefetchScalarGridSpec(
            num_scalar_prefetch=1,
            grid=(blocks // group,),
            in_specs=[rows(g) for g in range(group)]
            + [
                pl.BlockSpec((sensors, time_dev), lambda i, w: (0, 0)),
                pl.BlockSpec((group, win_rows, readings), lambda i, w: (i, 0, 0)),
                pl.BlockSpec((group, time_dev, readings), lambda i, w: (i, 0, 0)),
                pl.BlockSpec((blocks, readings), lambda i, w: (0, 0)),
                pl.BlockSpec((blocks, readings), lambda i, w: (0, 0)),
            ],
            out_specs=pl.BlockSpec((blocks, readings), lambda i, w: (0, 0)),
            scratch_shapes=[pltpu.VMEM((sensors, 2 * time_dev), BF16)],
        ),
        out_shape=jax.ShapeDtypeStruct((blocks, readings), F32),
        compiler_params=pltpu.CompilerParams(vmem_limit_bytes=48 << 20),
        name="image",
    )(
        window_index,
        *([sensor_kernel] * group),
        field,
        sensor_weights,
        time_weights,
        noise_var,
        value,
    )


def everywhere_body(n_sensor, n_tm, x_ref, out_ref, send_tm, recv_tm, send_sensor, recv_sensor):
    here, time = lax.axis_index("sensor"), lax.axis_index("tm")
    mesh_id = pl.DeviceIdType.MESH
    barrier = pltpu.get_barrier_semaphore()
    for d in range(1, n_tm):
        peer = (here, lax.rem(time + d, n_tm))
        pl.semaphore_signal(barrier, inc=1, device_id=peer, device_id_type=mesh_id)
    for d in range(1, n_sensor):
        peer = (lax.rem(here + d, n_sensor), time)
        pl.semaphore_signal(barrier, inc=1, device_id=peer, device_id_type=mesh_id)
    pl.semaphore_wait(barrier, n_tm - 1 + n_sensor - 1)

    copies = []
    for d in range(1, n_tm):
        copies.append(
            pltpu.make_async_remote_copy(
                src_ref=x_ref,
                dst_ref=out_ref.at[here * n_tm + time],
                send_sem=send_tm.at[d - 1],
                recv_sem=recv_tm.at[d - 1],
                device_id=(here, lax.rem(time + d, n_tm)),
                device_id_type=mesh_id,
            )
        )
        copies[-1].start()
    out_ref[here * n_tm + time] = x_ref[...]
    for copy in copies:
        copy.wait()
    row = out_ref.at[pl.ds(here * n_tm, n_tm)]
    copies = []
    for d in range(1, n_sensor):
        copies.append(
            pltpu.make_async_remote_copy(
                src_ref=row,
                dst_ref=row,
                send_sem=send_sensor.at[d - 1],
                recv_sem=recv_sensor.at[d - 1],
                device_id=(lax.rem(here + d, n_sensor), time),
                device_id_type=mesh_id,
            )
        )
        copies[-1].start()
    for copy in copies:
        copy.wait()


def gather_everywhere(n_sensor, n_tm, x, collective_id):
    dma = pltpu.SemaphoreType.DMA
    return pl.pallas_call(
        functools.partial(everywhere_body, n_sensor, n_tm),
        in_specs=[pl.BlockSpec(memory_space=pltpu.VMEM)],
        out_specs=pl.BlockSpec(memory_space=pltpu.VMEM),
        out_shape=jax.ShapeDtypeStruct((n_sensor * n_tm,) + x.shape, x.dtype),
        scratch_shapes=[
            dma((n_tm - 1,)),
            dma((n_tm - 1,)),
            dma((n_sensor - 1,)),
            dma((n_sensor - 1,)),
        ],
        compiler_params=pltpu.CompilerParams(
            collective_id=collective_id, has_side_effects=True, vmem_limit_bytes=40 << 20
        ),
        name="everywhere",
    )(x)


def on_device(
    n_sensor,
    n_tm,
    readings,
    noise_var,
    sensor_weights,
    time_weights,
    window_index,
    sensor_kernel,
    time_kernel,
):
    sensor_dev = sensor_kernel.shape[0]
    win_rows = sensor_weights.shape[1]
    blocks = readings.shape[0]
    mine = lax.axis_index("sensor")

    def everywhere(x, collective_id):
        return gather_everywhere(n_sensor, n_tm, x, collective_id)

    pack = lax.all_gather(
        compact(window_index, sensor_weights, time_weights), "tm", axis=0, tiled=False
    )
    inverse = inverse_of(
        noise_var, sensor_weights, time_weights, window_index, sensor_kernel, time_kernel
    )
    start = everywhere(jnp.concatenate([readings, inverse], axis=0), 1)
    windows = pack[:, 10, :, 0].astype(jnp.int32).reshape(-1)
    mixed = mix_times(pack, time_kernel)
    residual_all, inverse_all = start[:, :blocks], start[:, blocks:]
    direction_all = inverse_all * residual_all
    direction = inverse * readings
    inner = jnp.sum(residual_all * direction_all)

    def operator_apply(values_all, values):
        own = lax.dynamic_slice_in_dim(values_all, mine * n_tm, n_tm, 0)
        field = field_of(windows, pack, own, mixed, sensor_dev, win_rows)
        field = lax.all_gather(field, "sensor", axis=0, tiled=True)
        return image_of(
            window_index, sensor_kernel, field, sensor_weights, time_weights, noise_var, values
        )

    image = operator_apply(direction_all, direction)
    image_all = everywhere(image, 2)
    step_size = inner / jnp.sum(direction_all * image_all)
    solution = step_size * direction
    residual = readings - step_size * image
    residual_all = residual_all - step_size * image_all
    precond_all = inverse_all * residual_all
    inner_next = jnp.sum(residual_all * precond_all)
    ratio = inner_next / inner
    direction = inverse * residual + ratio * direction
    direction_all = precond_all + ratio * direction_all
    inner = inner_next

    image = operator_apply(direction_all, direction)
    curve = jnp.sum(everywhere(direction * image, 2))
    step_size = inner / curve
    return solution + step_size * direction, residual - step_size * image


def solution(mesh):
    in_specs = (
        P(("sensor", "tm"), None),
        P(("sensor", "tm"), None),
        P(("sensor", "tm"), None, None),
        P(("sensor", "tm"), None, None),
        P(("sensor", "tm")),
        P("sensor", None),
        P("tm", None),
    )
    out_specs = (P(("sensor", "tm"), None), P(("sensor", "tm"), None))
    return jax.shard_map(
        functools.partial(on_device, mesh.shape["sensor"], mesh.shape["tm"]),
        mesh=mesh,
        in_specs=in_specs,
        out_specs=out_specs,
        check_vma=False,
    )
```

```python
import functools

import jax
import jax.numpy as jnp
from jax import lax
from jax.experimental import pallas as pl
from jax.experimental.pallas import tpu as pltpu
from jax.sharding import PartitionSpec as P

PRECISE = lax.Precision.HIGHEST
F32 = jnp.float32
BF16 = jnp.bfloat16
TAPS = 4
FIELDS = 11


def split(x):
    hi = x.astype(BF16)
    return hi, (x - hi.astype(F32)).astype(BF16)


def dense(taps, first, rows):
    place = lax.broadcasted_iota(jnp.int32, (rows, first.shape[-1]), 0) - first
    out = jnp.where(place == TAPS - 1, taps[TAPS - 1], 0.0)
    for k in range(TAPS - 2, -1, -1):
        out = jnp.where(place == k, taps[k], out)
    return out


def compact_body(group, win_ref, sensor_ref, time_ref, pack_ref):
    step = pl.program_id(0)
    for g in range(group):
        row = pl.ds(step * group + g, 1)
        for ref, taps_at, first_at in ((time_ref, 0, 8), (sensor_ref, TAPS, 9)):
            tile = ref[g]
            ids = lax.broadcasted_iota(jnp.int32, tile.shape, 0)
            first = jnp.min(
                jnp.where(tile != 0.0, ids, tile.shape[0]), axis=0, keepdims=True
            )
            place = ids - first
            for k in range(TAPS):
                pack_ref[taps_at + k, row, :] = jnp.sum(
                    jnp.where(place == k, tile, 0.0), axis=0, keepdims=True
                )
            pack_ref[first_at, row, :] = first.astype(F32)
        window = win_ref[step * group + g]
        pack_ref[10, row, :] = jnp.full((1, tile.shape[1]), window, jnp.int32).astype(F32)


def compact(window_index, sensor_weights, time_weights):
    blocks, win_rows, readings = sensor_weights.shape
    time_dev = time_weights.shape[1]
    group = 4
    return pl.pallas_call(
        functools.partial(compact_body, group),
        grid_spec=pltpu.PrefetchScalarGridSpec(
            num_scalar_prefetch=1,
            grid=(blocks // group,),
            in_specs=[
                pl.BlockSpec((group, win_rows, readings), lambda i, w: (i, 0, 0)),
                pl.BlockSpec((group, time_dev, readings), lambda i, w: (i, 0, 0)),
            ],
            out_specs=pl.BlockSpec((FIELDS, blocks, readings), lambda i, w: (0, 0, 0)),
        ),
        out_shape=jax.ShapeDtypeStruct((FIELDS, blocks, readings), F32),
        name="compact",
    )(window_index, sensor_weights, time_weights)


def inverse_body(group, place_ref, *refs):
    squares = refs[:group]
    time_square, sensor_ref, time_ref, noise_ref, inverse_ref = refs[group:]
    step = pl.program_id(0)
    for g in range(group):
        block = step * group + g
        row = pl.ds(block, 1)
        weights = sensor_ref[g]
        odd = (place_ref[block] % 2).astype(F32)
        both = jnp.concatenate([weights * (1.0 - odd), weights * odd], axis=0)
        mixed = jnp.dot(squares[g][...], both, precision=PRECISE, preferred_element_type=F32)
        sensor_quad = jnp.sum(weights * mixed, axis=0, keepdims=True)
        taps = time_ref[g]
        mixed = jnp.dot(time_square[...], taps, precision=PRECISE, preferred_element_type=F32)
        time_quad = jnp.sum(taps * mixed, axis=0, keepdims=True)
        inverse_ref[row, :] = 1.0 / (sensor_quad * time_quad + noise_ref[row, :])


def inverse_of(noise_var, sensor_weights, time_weights, window_index, sensor_kernel, time_kernel):
    blocks, win_rows, readings = sensor_weights.shape
    time_dev = time_weights.shape[1]
    sensor_dev = sensor_kernel.shape[0]
    group = 4
    place = jnp.concatenate(
        [
            window_index,
            lax.axis_index("sensor")[None].astype(jnp.int32),
            lax.axis_index("tm")[None].astype(jnp.int32),
        ]
    )

    def square(g):
        def where(i, p):
            window = p[i * group + g]
            return window, (p[blocks] * sensor_dev + window * win_rows) // (2 * win_rows)

        return pl.BlockSpec((win_rows, 2 * win_rows), where)

    return pl.pallas_call(
        functools.partial(inverse_body, group),
        grid_spec=pltpu.PrefetchScalarGridSpec(
            num_scalar_prefetch=1,
            grid=(blocks // group,),
            in_specs=[square(g) for g in range(group)]
            + [
                pl.BlockSpec((time_dev, time_dev), lambda i, p: (0, p[blocks + 1])),
                pl.BlockSpec((group, win_rows, readings), lambda i, p: (i, 0, 0)),
                pl.BlockSpec((group, time_dev, readings), lambda i, p: (i, 0, 0)),
                pl.BlockSpec((blocks, readings), lambda i, p: (0, 0)),
            ],
            out_specs=pl.BlockSpec((blocks, readings), lambda i, p: (0, 0)),
        ),
        out_shape=jax.ShapeDtypeStruct((blocks, readings), F32),
        cost_estimate=pl.CostEstimate(
            flops=12 * blocks * time_dev * time_dev * readings,
            bytes_accessed=4 * blocks * time_dev * readings * 4,
            transcendentals=0,
        ),
        name="inverse",
    )(place, *([sensor_kernel] * group), time_kernel, sensor_weights, time_weights, noise_var)


def times_body(pack_ref, kernel_ref, mixed_ref):
    time_dev = kernel_ref.shape[0]
    blocks, readings = pack_ref.shape[2:]
    k_hi, k_lo = split(kernel_ref[...])
    for b in range(0, blocks, 2):
        tiles = []
        for c in (b, b + 1):
            row = slice(c, c + 1)
            taps = [pack_ref[0, k, row, :] for k in range(TAPS)]
            tiles.append(dense(taps, pack_ref[0, 8, row, :].astype(jnp.int32), time_dev))
        w_hi, w_lo = split(jnp.concatenate(tiles, axis=1))
        dot = functools.partial(jnp.dot, preferred_element_type=F32)
        hi, lo = split(dot(k_hi, w_hi) + (dot(k_hi, w_lo) + dot(k_lo, w_hi)))
        for n in range(2):
            part = slice(n * readings, (n + 1) * readings)
            mixed_ref[b + n, :, :readings] = hi[:, part]
            mixed_ref[b + n, :, readings:] = lo[:, part]


def mix_times(pack, time_kernel):
    n_tm, _, blocks, readings = pack.shape
    time_dev = time_kernel.shape[0]
    return pl.pallas_call(
        times_body,
        grid=(n_tm,),
        in_specs=[
            pl.BlockSpec((1, FIELDS, blocks, readings), lambda i: (i, 0, 0, 0)),
            pl.BlockSpec((time_dev, time_dev), lambda i: (0, i)),
        ],
        out_specs=pl.BlockSpec((blocks, time_dev, 2 * readings), lambda i: (i, 0, 0)),
        out_shape=jax.ShapeDtypeStruct((n_tm * blocks, time_dev, 2 * readings), BF16),
        compiler_params=pltpu.CompilerParams(vmem_limit_bytes=40 << 20),
        cost_estimate=pl.CostEstimate(
            flops=6 * n_tm * blocks * time_dev * time_dev * readings,
            bytes_accessed=4 * n_tm * blocks * time_dev * readings,
            transcendentals=0,
        ),
        name="mix_times",
    )(pack, time_kernel)


def field_body(win_rows, win_ref, pack_ref, value_ref, mixed_ref, field_ref):
    step = pl.program_id(0)
    blocks, readings = pack_ref.shape[2:]

    @pl.when(step == 0)
    def _():
        field_ref[...] = jnp.zeros_like(field_ref)

    for b in range(blocks):
        row = slice(b, b + 1)
        value = value_ref[0, row, :]
        taps = [pack_ref[0, TAPS + k, row, :] * value for k in range(TAPS)]
        hi, lo = split(dense(taps, pack_ref[0, 9, row, :].astype(jnp.int32), win_rows))
        left = jnp.concatenate(
            [
                jnp.concatenate([hi, hi], axis=1),
                jnp.concatenate([lo, jnp.zeros_like(lo)], axis=1),
            ],
            axis=0,
        )
        out = lax.dot_general(
            left, mixed_ref[b], (((1,), (1,)), ((), ())), preferred_element_type=F32
        )
        start = pl.multiple_of(win_ref[step * blocks + b] * win_rows, win_rows)
        field_ref[pl.ds(start, win_rows), :] += out[:win_rows] + out[win_rows:]


def field_of(windows, pack, values, mixed, sensor_dev, win_rows):
    n_tm, _, blocks, readings = pack.shape
    time_dev = mixed.shape[1]
    return pl.pallas_call(
        functools.partial(field_body, win_rows),
        grid_spec=pltpu.PrefetchScalarGridSpec(
            num_scalar_prefetch=1,
            grid=(n_tm,),
            in_specs=[
                pl.BlockSpec((1, FIELDS, blocks, readings), lambda i, w: (i, 0, 0, 0)),
                pl.BlockSpec((1, blocks, readings), lambda i, w: (i, 0, 0)),
                pl.BlockSpec((blocks, time_dev, 2 * readings), lambda i, w: (i, 0, 0)),
            ],
            out_specs=pl.BlockSpec((sensor_dev, time_dev), lambda i, w: (0, 0)),
        ),
        out_shape=jax.ShapeDtypeStruct((sensor_dev, time_dev), F32),
        compiler_params=pltpu.CompilerParams(vmem_limit_bytes=40 << 20),
        name="field",
    )(windows, pack, values, mixed)


def image_body(group, chunk, win_ref, *refs):
    kernels = refs[:group]
    field_ref, sensor_ref, time_ref, noise_ref, value_ref, image_ref, halves = refs[group:]
    step = pl.program_id(0)
    time_dev = field_ref.shape[1]
    win_rows = sensor_ref.shape[1]
    sensors = field_ref.shape[0]
    dot = functools.partial(jnp.dot, preferred_element_type=F32)

    @pl.when(step == 0)
    def _():
        for k in range(0, sensors, chunk):
            hi, lo = split(field_ref[k : k + chunk, :])
            halves[k : k + chunk, :time_dev] = hi
            halves[k : k + chunk, time_dev:] = lo

    total = jnp.zeros((group * win_rows, 2 * time_dev), F32)
    extra = jnp.zeros((group * win_rows, time_dev), F32)
    for k in range(0, sensors, chunk):
        left = jnp.concatenate([ref[:, k : k + chunk] for ref in kernels], axis=0)
        hi, lo = split(left)
        total = total + dot(hi, halves[k : k + chunk, :])
        extra = extra + dot(lo, halves[k : k + chunk, :time_dev])
    smooth = total[:, :time_dev] + (total[:, time_dev:] + extra)
    for g in range(group):
        row = pl.ds(step * group + g, 1)
        interp = jnp.dot(
            smooth[g * win_rows : (g + 1) * win_rows],
            time_ref[g],
            precision=PRECISE,
            preferred_element_type=F32,
        )
        image_ref[row, :] = (
            jnp.sum(sensor_ref[g] * interp, axis=0, keepdims=True)
            + noise_ref[row, :] * value_ref[row, :]
        )


def image_of(window_index, sensor_kernel, field, sensor_weights, time_weights, noise_var, value):
    blocks, win_rows, readings = sensor_weights.shape
    sensors, time_dev = field.shape
    group = 4
    chunk = 512

    def rows(g):
        return pl.BlockSpec((win_rows, sensors), lambda i, w: (w[i * group + g], 0))

    return pl.pallas_call(
        functools.partial(image_body, group, chunk),
        grid_spec=pltpu.PrefetchScalarGridSpec(
            num_scalar_prefetch=1,
            grid=(blocks // group,),
            in_specs=[rows(g) for g in range(group)]
            + [
                pl.BlockSpec((sensors, time_dev), lambda i, w: (0, 0)),
                pl.BlockSpec((group, win_rows, readings), lambda i, w: (i, 0, 0)),
                pl.BlockSpec((group, time_dev, readings), lambda i, w: (i, 0, 0)),
                pl.BlockSpec((blocks, readings), lambda i, w: (0, 0)),
                pl.BlockSpec((blocks, readings), lambda i, w: (0, 0)),
            ],
            out_specs=pl.BlockSpec((blocks, readings), lambda i, w: (0, 0)),
            scratch_shapes=[pltpu.VMEM((sensors, 2 * time_dev), BF16)],
        ),
        out_shape=jax.ShapeDtypeStruct((blocks, readings), F32),
        compiler_params=pltpu.CompilerParams(vmem_limit_bytes=48 << 20),
        name="image",
    )(
        window_index,
        *([sensor_kernel] * group),
        field,
        sensor_weights,
        time_weights,
        noise_var,
        value,
    )


def everywhere_body(n_sensor, n_tm, x_ref, out_ref, send_tm, recv_tm, send_sensor, recv_sensor):
    here, time = lax.axis_index("sensor"), lax.axis_index("tm")
    mesh_id = pl.DeviceIdType.MESH
    barrier = pltpu.get_barrier_semaphore()
    for d in range(1, n_tm):
        peer = (here, lax.rem(time + d, n_tm))
        pl.semaphore_signal(barrier, inc=1, device_id=peer, device_id_type=mesh_id)
    for d in range(1, n_sensor):
        peer = (lax.rem(here + d, n_sensor), time)
        pl.semaphore_signal(barrier, inc=1, device_id=peer, device_id_type=mesh_id)
    pl.semaphore_wait(barrier, n_tm - 1 + n_sensor - 1)

    copies = []
    for d in range(1, n_tm):
        copies.append(
            pltpu.make_async_remote_copy(
                src_ref=x_ref,
                dst_ref=out_ref.at[here * n_tm + time],
                send_sem=send_tm.at[d - 1],
                recv_sem=recv_tm.at[d - 1],
                device_id=(here, lax.rem(time + d, n_tm)),
                device_id_type=mesh_id,
            )
        )
        copies[-1].start()
    out_ref[here * n_tm + time] = x_ref[...]
    for copy in copies:
        copy.wait()
    row = out_ref.at[pl.ds(here * n_tm, n_tm)]
    copies = []
    for d in range(1, n_sensor):
        copies.append(
            pltpu.make_async_remote_copy(
                src_ref=row,
                dst_ref=row,
                send_sem=send_sensor.at[d - 1],
                recv_sem=recv_sensor.at[d - 1],
                device_id=(lax.rem(here + d, n_sensor), time),
                device_id_type=mesh_id,
            )
        )
        copies[-1].start()
    for copy in copies:
        copy.wait()


def gather_everywhere(n_sensor, n_tm, x, collective_id):
    dma = pltpu.SemaphoreType.DMA
    return pl.pallas_call(
        functools.partial(everywhere_body, n_sensor, n_tm),
        in_specs=[pl.BlockSpec(memory_space=pltpu.VMEM)],
        out_specs=pl.BlockSpec(memory_space=pltpu.VMEM),
        out_shape=jax.ShapeDtypeStruct((n_sensor * n_tm,) + x.shape, x.dtype),
        scratch_shapes=[
            dma((n_tm - 1,)),
            dma((n_tm - 1,)),
            dma((n_sensor - 1,)),
            dma((n_sensor - 1,)),
        ],
        compiler_params=pltpu.CompilerParams(
            collective_id=collective_id, has_side_effects=True, vmem_limit_bytes=40 << 20
        ),
        name="everywhere",
    )(x)


def beside_body(n_sensor, x_ref, out_ref, send, recv):
    here, time = lax.axis_index("sensor"), lax.axis_index("tm")
    mesh_id = pl.DeviceIdType.MESH
    peers = [(lax.rem(here + d, n_sensor), time) for d in range(1, n_sensor)]
    barrier = pltpu.get_barrier_semaphore()
    for peer in peers:
        pl.semaphore_signal(barrier, inc=1, device_id=peer, device_id_type=mesh_id)
    pl.semaphore_wait(barrier, n_sensor - 1)
    copies = [
        pltpu.make_async_remote_copy(
            src_ref=x_ref,
            dst_ref=out_ref.at[here],
            send_sem=send.at[d],
            recv_sem=recv.at[d],
            device_id=peer,
            device_id_type=mesh_id,
        )
        for d, peer in enumerate(peers)
    ]
    for copy in copies:
        copy.start()
    out_ref[here] = x_ref[...]
    for copy in copies:
        copy.wait()


def gather_beside(n_sensor, x):
    dma = pltpu.SemaphoreType.DMA
    return pl.pallas_call(
        functools.partial(beside_body, n_sensor),
        in_specs=[pl.BlockSpec(memory_space=pltpu.VMEM)],
        out_specs=pl.BlockSpec(memory_space=pltpu.VMEM),
        out_shape=jax.ShapeDtypeStruct((n_sensor,) + x.shape, x.dtype),
        scratch_shapes=[dma((n_sensor - 1,)), dma((n_sensor - 1,))],
        compiler_params=pltpu.CompilerParams(
            collective_id=3, has_side_effects=True, vmem_limit_bytes=40 << 20
        ),
        name="beside",
    )(x).reshape(n_sensor * x.shape[0], x.shape[1])


def on_device(
    n_sensor,
    n_tm,
    readings,
    noise_var,
    sensor_weights,
    time_weights,
    window_index,
    sensor_kernel,
    time_kernel,
):
    sensor_dev = sensor_kernel.shape[0]
    win_rows = sensor_weights.shape[1]
    blocks = readings.shape[0]
    mine = lax.axis_index("sensor")

    def everywhere(x, collective_id):
        return gather_everywhere(n_sensor, n_tm, x, collective_id)

    pack = lax.all_gather(
        compact(window_index, sensor_weights, time_weights), "tm", axis=0, tiled=False
    )
    inverse = inverse_of(
        noise_var, sensor_weights, time_weights, window_index, sensor_kernel, time_kernel
    )
    start = everywhere(jnp.concatenate([readings, inverse], axis=0), 1)
    windows = pack[:, 10, :, 0].astype(jnp.int32).reshape(-1)
    mixed = mix_times(pack, time_kernel)
    residual_all, inverse_all = start[:, :blocks], start[:, blocks:]
    direction_all = inverse_all * residual_all
    direction = inverse * readings
    inner = jnp.sum(residual_all * direction_all)

    def operator_apply(values_all, values):
        own = lax.dynamic_slice_in_dim(values_all, mine * n_tm, n_tm, 0)
        field = field_of(windows, pack, own, mixed, sensor_dev, win_rows)
        field = gather_beside(n_sensor, field)
        return image_of(
            window_index, sensor_kernel, field, sensor_weights, time_weights, noise_var, values
        )

    image = operator_apply(direction_all, direction)
    image_all = everywhere(image, 2)
    step_size = inner / jnp.sum(direction_all * image_all)
    solution = step_size * direction
    residual = readings - step_size * image
    residual_all = residual_all - step_size * image_all
    precond_all = inverse_all * residual_all
    inner_next = jnp.sum(residual_all * precond_all)
    ratio = inner_next / inner
    direction = inverse * residual + ratio * direction
    direction_all = precond_all + ratio * direction_all
    inner = inner_next

    image = operator_apply(direction_all, direction)
    curve = jnp.sum(everywhere(direction * image, 2))
    step_size = inner / curve
    return solution + step_size * direction, residual - step_size * image


def solution(mesh):
    in_specs = (
        P(("sensor", "tm"), None),
        P(("sensor", "tm"), None),
        P(("sensor", "tm"), None, None),
        P(("sensor", "tm"), None, None),
        P(("sensor", "tm")),
        P("sensor", None),
        P("tm", None),
    )
    out_specs = (P(("sensor", "tm"), None), P(("sensor", "tm"), None))
    return jax.shard_map(
        functools.partial(on_device, mesh.shape["sensor"], mesh.shape["tm"]),
        mesh=mesh,
        in_specs=in_specs,
        out_specs=out_specs,
        check_vma=False,
    )
```
